128 devices in a mesh: row: 8 (over z_lo, y), col: 16 (over z_hi, x, core).
Axes of the slice: x: 4, y: 4, z: 4 (z_hi: 2, z_lo: 2; z = z_hi * 2 + z_lo), core: 2. Of those that a mesh axis runs over, the one named last changes fastest.
Arguments:
- queries: bfloat16 [16384, 512], P(('row', 'col')), may hold values from -6 to 6
- keys: bfloat16 [8192, 512], P(('col', 'row')), may hold values from -6 to 6
- values: bfloat16 [8192, 512], P(('col', 'row')), may hold values from -6 to 6
- outputs: bfloat16 [16384, 512], P(('row', 'col')), may hold values from -3 to 3
- d_out: bfloat16 [16384, 512], P(('row', 'col')), may hold values from -816 to 816
- lse: float32 [4, 16384], P(None, ('row', 'col')), as said below
Outputs:
- grad_queries: float32 [16384, 512], P(('row', 'col'))
- grad_keys: float32 [8192, 512], P(('col', 'row'))
- grad_values: float32 [8192, 512], P(('col', 'row'))
The draws below stay inside these ranges and needn't reach their ends.
Inputs may be any that keep to these rules, and one draw needn't show every extreme that they name: Each entry of lse exceeds the natural logarithm of 8192 by 0 to 3.
All inputs are finite; a program needn't handle non-finite values.
Results may differ from the reference program's by a relative error of at most 0.0047.
Values may be sent and summed in bfloat16 or wider, within the bound.
No kernel may reach another device: no remote copies, remote signals or barrier semaphores. Data moves between devices by JAX's collectives and lax.ppermute only.
A program may use at most 128 MiB of HBM per device.

```python
import math
import jax
import jax.numpy as jnp
from jax import lax

H = 4
DH = 128
SQ = 16384
SK = 8192


def draw_lse(key, part):
    key = jax.random.fold_in(key, 7)
    lowest = 0.5
    highest = 2.5
    spread = jax.random.uniform(key, (H, SQ), jnp.float32)
    return (math.log(SK) + lowest + spread * (highest - lowest)).astype(jnp.float32)


def block_scale(key, shape, cuts, low, top_value):
    def one(axis_at, shards_of):
        draws = jax.random.uniform(jax.random.fold_in(jax.random.fold_in(key, 6), axis_at), (shards_of,), jnp.float32, low / len(cuts), top_value / len(cuts))
        return jnp.repeat(jnp.exp(draws), shape[axis_at] // shards_of).reshape((-1,) + (1,) * (len(shape) - axis_at - 1))

    gain = one(*cuts[0])
    for cut in cuts[1:]:
        gain = gain * one(*cut)
    return gain


def scatter_about(own_key, extent, scale, limit, shards=(), kind=jnp.bfloat16):
    factor_of = block_scale(own_key, extent, shards, -0.22, 0.18) if shards else 1.0
    values = jax.random.normal(own_key, extent, jnp.float32) * scale * factor_of
    return jnp.minimum(jnp.maximum(values, -limit), limit).astype(kind)


def setup_inputs(seed: int = 0) -> dict:
    key_of = jax.random.split(jax.random.key(seed), 7)
    queries = scatter_about(key_of[0], (SQ, H * DH), 1.0, 6.0, ((0, 128),))
    keys = scatter_about(key_of[1], (SK, H * DH), 1.0, 6.0, ((0, 128),))
    values = scatter_about(key_of[2], (SK, H * DH), 1.0, 6.0, ((0, 128),))
    outputs = scatter_about(key_of[3], (SQ, H * DH), 0.5, 3.0, ((0, 128),))
    d_out = scatter_about(key_of[4], (SQ, H * DH), (SK // 64 + 8), 816.0, ((0, 128),))
    lse = draw_lse(jax.random.fold_in(key_of[6], 71), 0)
    return {"queries": queries, "keys": keys, "values": values, "outputs": outputs, "d_out": d_out, "lse": lse}


def head_terms(query_rows, dout_rows, lse_rows, delta_rows, key_cols, value_cols, factor):
    scores = jnp.dot(query_rows, key_cols.T, preferred_element_type=jnp.float32) * factor
    probs = jnp.exp(scores - lse_rows[:, None])
    dprobs = jnp.dot(dout_rows, value_cols.T, preferred_element_type=jnp.float32)
    dscores = (probs * (dprobs - delta_rows[:, None]) * factor).astype(jnp.bfloat16)
    grad_query = jnp.dot(dscores, key_cols, preferred_element_type=jnp.float32)
    grad_key = jnp.dot(dscores.T, query_rows, preferred_element_type=jnp.float32)
    grad_value = jnp.dot(probs.astype(jnp.bfloat16).T, dout_rows, preferred_element_type=jnp.float32)
    return (grad_query, grad_key, grad_value)

def reference(queries, keys, values, outputs, d_out, lse):
    factor = 1.0 / math.sqrt(DH)
    block = math.gcd(SQ, 512)
    block_count = SQ // block
    delta = lax.optimization_barrier(jnp.sum((d_out.astype(jnp.float32) * outputs.astype(jnp.float32)).reshape(SQ, H, DH), axis=2)).T

    def advance(totals, index):
        first_row = index * block
        query_rows = lax.dynamic_slice_in_dim(queries, first_row, block, 0)
        dout_rows = lax.dynamic_slice_in_dim(d_out, first_row, block, 0)
        lse_rows = lax.dynamic_slice_in_dim(lse, first_row, block, 1)
        delta_rows = lax.dynamic_slice_in_dim(delta, first_row, block, 1)
        query_parts, key_parts, value_parts = ([], [], [])
        for head_index in range(H):
            low = head_index * DH
            high = low + DH
            grad_query, grad_key, grad_value = head_terms(query_rows[:, low:high], dout_rows[:, low:high], lse_rows[head_index], delta_rows[head_index], keys[:, low:high], values[:, low:high], factor)
            query_parts.append(grad_query)
            key_parts.append(grad_key)
            value_parts.append(grad_value)
        new_totals = (totals[0] + jnp.concatenate(key_parts, axis=1), totals[1] + jnp.concatenate(value_parts, axis=1))
        return (new_totals, jnp.concatenate(query_parts, axis=1))
    start_totals = (jnp.zeros((SK, H * DH), jnp.float32), jnp.zeros((SK, H * DH), jnp.float32))
    totals, query_blocks = lax.scan(advance, start_totals, jnp.arange(block_count, dtype=jnp.int32))
    return (query_blocks.reshape(SQ, H * DH), totals[0], totals[1])
```

```python
import functools
import math

import jax
import jax.numpy as jnp
from jax import lax
from jax.experimental import pallas as pl
from jax.experimental.pallas import tpu as pltpu
from jax.sharding import PartitionSpec as P

H = 4
DH = 128
AXES = ("row", "col")
F32 = jnp.float32
BF16 = jnp.bfloat16
QR = 128
KR = 64
AUX = 16
BLK = QR + KR + AUX
QS = 4 * QR
KS = 4 * KR
FACTOR = 1.0 / math.sqrt(DH)
LOG2E = math.log2(math.e)
VMEM = pl.BlockSpec(memory_space=pltpu.VMEM)
NT = (((1,), (1,)), ((), ()))


def linear(x, y, z, c):
    return ((z % 2) * 4 + y) * 16 + (z // 2) * 8 + x * 2 + c


def shift(value, dx=0, dy=0, dz=0, dc=0):
    pairs = []
    for x in range(4):
        for y in range(4):
            for z in range(4):
                for c in range(2):
                    there = linear((x + dx) % 4, (y + dy) % 4, (z + dz) % 4, c ^ dc)
                    pairs.append((linear(x, y, z, c), there))
    return lax.ppermute(value, AXES, pairs)


def three_parts(value):
    high = value.astype(BF16).astype(F32)
    rest = value - high
    middle = rest.astype(BF16).astype(F32)
    return [high, middle, rest - middle]


def pack_kernel(q_ref, k_ref, v_ref, o_ref, g_ref, lse_ref, *blocks):
    y = lax.axis_index("row") % 4
    for j, block in enumerate(blocks):
        head = lax.rem(y + j, 4)
        cols = pl.ds(pl.multiple_of(head * DH, DH), DH)
        g = g_ref[:, cols]
        block[:QR, :DH] = q_ref[:, cols]
        block[:QR, DH:] = g
        block[QR : QR + KR, :DH] = k_ref[:, cols]
        block[QR : QR + KR, DH:] = v_ref[:, cols]
        product = g.astype(F32) * o_ref[:, cols].astype(F32)
        delta = jnp.sum(product.T, axis=0, keepdims=True)
        both = jnp.concatenate([lse_ref[pl.ds(head, 1), :], delta], axis=1)
        rows = three_parts(both) + [jnp.zeros((AUX - 3, 2 * DH), F32)]
        block[QR + KR :, :] = jnp.concatenate(rows, axis=0).astype(BF16)


def join_kernel(b0, b1, b2, b3, q_out, kv_out):
    aux = []
    for j, block in enumerate((b0, b1, b2, b3)):
        q_out[j * QR : (j + 1) * QR, :] = block[:QR, :]
        kv_out[j * KR : (j + 1) * KR, :] = block[QR : QR + KR, :]
        aux.append(block[QR + KR :, :].astype(F32)[:3])
    aux.append(jnp.zeros((AUX - 12, 2 * DH), F32))
    q_out[QS:, :] = jnp.concatenate(aux, axis=0).astype(BF16)


def row_terms(q_ref):
    aux = q_ref[QS:, :].astype(F32)
    lse, delta = [], []
    for j in range(4):
        total = aux[3 * j : 3 * j + 1] + aux[3 * j + 1 : 3 * j + 2] + aux[3 * j + 2 : 3 * j + 3]
        lse.append(total[:, :DH])
        delta.append(total[:, DH:])
    return jnp.concatenate(lse, axis=1) * LOG2E, jnp.concatenate(delta, axis=1)


def attend_kernel(*refs):
    q_refs = refs[0:4]
    own_refs = refs[4:8]
    other_refs = refs[8:12]
    dq_own, dq_a, dq_b, dq_c, dkv_own, dkv_other = refs[12:18]
    kv, kt, dkv, dqt, terms = refs[18:]
    for i in range(4):
        kv[i * KS : (i + 1) * KS, :] = own_refs[i][...]
        kv[(4 + i) * KS : (5 + i) * KS, :] = other_refs[i][...]
    kt[...] = kv[:, :DH].T
    for b, q_ref in enumerate(q_refs):
        lse, delta = row_terms(q_ref)
        terms[b, 0:1, :] = lse
        terms[b, 1:2, :] = delta
    tile = 512
    for b, q_ref in enumerate(q_refs):

        def step(i, carry, b=b, q_ref=q_ref):
            rows = pl.ds(pl.multiple_of(i * tile, tile), tile)
            q = q_ref[:QS, :DH]
            g = q_ref[:QS, DH:]
            s = lax.dot_general(kv[rows, :DH], q, NT, preferred_element_type=F32)
            p = jnp.exp2(s * (FACTOR * LOG2E) - terms[b, 0:1, :])
            dp = lax.dot_general(kv[rows, DH:], g, NT, preferred_element_type=F32)
            ds = (p * (dp - terms[b, 1:2, :]) * FACTOR).astype(BF16)
            dv = jnp.dot(p.astype(BF16), g, preferred_element_type=F32)
            dk = jnp.dot(ds, q, preferred_element_type=F32)
            dq = jnp.dot(kt[:, rows], ds, preferred_element_type=F32)
            if b == 0:
                dkv[rows, :DH] = dk
                dkv[rows, DH:] = dv
            else:
                dkv[rows, :DH] += dk
                dkv[rows, DH:] += dv
            dqt[b] = jnp.where(i == 0, dq, dqt[b] + dq)
            return carry

        lax.fori_loop(0, 8 * KS // tile, step, 0)
    dq_own[...] = dqt[0].T
    for b, out in enumerate((dq_a, dq_b, dq_c)):
        out[...] = dqt[b + 1].T.astype(BF16)
    dkv_own[...] = dkv[: 4 * KS, :]
    dkv_other[...] = dkv[4 * KS :, :].astype(BF16)


def core_sum_kernel(own, other, s0, s1, s2, s3):
    for i, out in enumerate((s0, s1, s2, s3)):
        rows = slice(i * KS, (i + 1) * KS)
        out[...] = (own[rows, :] + other[rows, :].astype(F32)).astype(out.dtype)


def chip_sum_kernel(q0, q1, q2, q3, k0, k1, k2, k3, *outs):
    dq = q0[...] + q1[...].astype(F32) + q2[...].astype(F32) + q3[...].astype(F32)
    dkv = k0[...] + k1[...].astype(F32) + k2[...].astype(F32) + k3[...].astype(F32)
    for j, out in enumerate(outs):
        part = dq[j * QR : (j + 1) * QR]
        wide = jnp.concatenate([part[: QR // 2], part[QR // 2 :]], axis=1)
        out[:KR, :] = wide.astype(out.dtype)
        out[KR:, :] = dkv[j * KR : (j + 1) * KR].astype(out.dtype)


def unpack_kernel(b0, b1, b2, b3, dq, dk, dv):
    y = lax.axis_index("row") % 4
    for j, block in enumerate((b0, b1, b2, b3)):
        cols = pl.ds(pl.multiple_of(lax.rem(y + j, 4) * DH, DH), DH)
        dq[: QR // 2, cols] = block[:KR, :DH].astype(F32)
        dq[QR // 2 :, cols] = block[:KR, DH:].astype(F32)
        dk[:, cols] = block[KR:, :DH].astype(F32)
        dv[:, cols] = block[KR:, DH:].astype(F32)


def call(kernel, outs, args, scratch=(), flops=0):
    total = sum(a.size * a.dtype.itemsize for a in args) + sum(
        math.prod(shape) * jnp.dtype(kind).itemsize for shape, kind in outs
    )
    return pl.pallas_call(
        kernel,
        out_shape=[jax.ShapeDtypeStruct(shape, kind) for shape, kind in outs],
        in_specs=[VMEM] * len(args),
        out_specs=[VMEM] * len(outs),
        scratch_shapes=list(scratch),
        compiler_params=pltpu.CompilerParams(vmem_limit_bytes=40 * 1024 * 1024),
        cost_estimate=pl.CostEstimate(flops=flops, bytes_accessed=total, transcendentals=0),
    )(*args)


def per_device(queries, keys, values, outputs, d_out, lse):
    with jax.named_scope("pack"):
        blocks = call(
            pack_kernel, [((BLK, 2 * DH), BF16)] * 4, (queries, keys, values, outputs, d_out, lse)
        )
    with jax.named_scope("heads_over_y"):
        blocks = [blocks[0]] + [shift(blocks[j], dy=j) for j in (1, 2, 3)]
    with jax.named_scope("join"):
        q, kv = call(
            join_kernel, [((QS + AUX, 2 * DH), BF16), ((KS, 2 * DH), BF16)], blocks
        )
    with jax.named_scope("keys_over_z"):
        own = [kv] + [shift(kv, dz=d) for d in (1, 3, 2)]
        other = [shift(part, dc=1) for part in own]
    with jax.named_scope("queries_over_x"):
        qs = [q] + [shift(q, dx=d) for d in (1, 3, 2)]
    with jax.named_scope("attend"):
        dq0, dq1, dq2, dq3, dkv_own, dkv_other = call(
            attend_kernel,
            [((QS, DH), F32)]
            + [((QS, DH), BF16)] * 3
            + [((4 * KS, 2 * DH), F32), ((4 * KS, 2 * DH), BF16)],
            qs + own + other,
            scratch=[
                pltpu.VMEM((8 * KS, 2 * DH), BF16),
                pltpu.VMEM((DH, 8 * KS), BF16),
                pltpu.VMEM((8 * KS, 2 * DH), F32),
                pltpu.VMEM((4, DH, QS), F32),
                pltpu.VMEM((4, 8, QS), F32),
            ],
            flops=10 * 2048 * 2048 * 128,
        )
    with jax.named_scope("sum_queries_over_x"):
        dqs = [dq0, shift(dq1, dx=3), shift(dq2, dx=1), shift(dq3, dx=2)]
    with jax.named_scope("sum_keys_over_core"):
        dkv_other = shift(dkv_other, dc=1)
        parts = call(
            core_sum_kernel,
            [((KS, 2 * DH), F32)] + [((KS, 2 * DH), BF16)] * 3,
            (dkv_own, dkv_other),
        )
    with jax.named_scope("sum_keys_over_z"):
        dkvs = [parts[0]] + [shift(parts[1], dz=3), shift(parts[2], dz=1), shift(parts[3], dz=2)]
    with jax.named_scope("chip_sum"):
        backs = call(
            chip_sum_kernel,
            [((2 * KR, 2 * DH), F32)] + [((2 * KR, 2 * DH), BF16)] * 3,
            dqs + dkvs,
        )
    with jax.named_scope("back_over_y"):
        backs = [backs[0]] + [shift(backs[j], dy=4 - j) for j in (1, 2, 3)]
    with jax.named_scope("unpack"):
        return tuple(
            call(
                unpack_kernel,
                [((QR, H * DH), F32), ((KR, H * DH), F32), ((KR, H * DH), F32)],
                backs,
            )
        )


def solution(mesh):
    return jax.shard_map(
        per_device,
        mesh=mesh,
        in_specs=(
            P(("row", "col"), None),
            P(("col", "row"), None),
            P(("col", "row"), None),
            P(("row", "col"), None),
            P(("row", "col"), None),
            P(None, ("row", "col")),
        ),
        out_specs=(P(("row", "col"), None), P(("col", "row"), None), P(("col", "row"), None)),
        check_vma=False,
    )
```

```python
import functools
import math

import jax
import jax.numpy as jnp
from jax import lax
from jax.experimental import pallas as pl
from jax.experimental.pallas import tpu as pltpu
from jax.sharding import PartitionSpec as P

H = 4
DH = 128
AXES = ("row", "col")
F32 = jnp.float32
BF16 = jnp.bfloat16
QR = 128
KR = 64
AUX = 16
TILE = 512
BLK = QR + KR + AUX
QS = 4 * QR
KS = 4 * KR
FACTOR = 1.0 / math.sqrt(DH)
LOG2E = math.log2(math.e)
VMEM = pl.BlockSpec(memory_space=pltpu.VMEM)
NT = (((1,), (1,)), ((), ()))


def linear(x, y, z, c):
    return ((z % 2) * 4 + y) * 16 + (z // 2) * 8 + x * 2 + c


def move(value, target):
    pairs = []
    for x in range(4):
        for y in range(4):
            for z in range(4):
                for c in range(2):
                    pairs.append((linear(x, y, z, c), linear(*target(x, y, z, c))))
    return lax.ppermute(value, AXES, pairs)


def other_core(value):
    return move(value, lambda x, y, z, c: (x, y, z, 1 - c))


def along_y(value, step):
    return move(value, lambda x, y, z, c: (x, (y + step) % 4, z, c))


def partner(place, core, kind):
    if kind == 2:
        return (place + 2) % 4
    up = place % 2 == (kind + core) % 2
    return (place + (1 if up else -1)) % 4


def swap_x(value, kind):
    return move(value, lambda x, y, z, c: (partner(x, c, kind), y, z, c))


def swap_z(value, kind):
    return move(value, lambda x, y, z, c: (x, y, partner(z, c, kind), c))


def three_parts(value):
    high = value.astype(BF16).astype(F32)
    rest = value - high
    middle = rest.astype(BF16).astype(F32)
    return [high, middle, rest - middle]


def pack_kernel(steps, *refs):
    blocks, bufs, sem = refs[6:-7], refs[-7:-1], refs[-1]
    copies = [pltpu.make_async_copy(refs[i], bufs[i], sem.at[i]) for i in range(6)]
    for copy in copies:
        copy.start()
    for copy in copies:
        copy.wait()
    q_ref, k_ref, v_ref, o_ref, g_ref, lse_ref = bufs
    y = lax.axis_index("row") % 4
    for step, block in zip(steps, blocks):
        head = lax.rem(y + step, 4)
        cols = pl.ds(pl.multiple_of(head * DH, DH), DH)
        g = g_ref[:, cols]
        block[:QR, :DH] = q_ref[:, cols]
        block[:QR, DH:] = g
        block[QR : QR + KR, :DH] = k_ref[:, cols]
        block[QR : QR + KR, DH:] = v_ref[:, cols]
        product = g.astype(F32) * o_ref[:, cols].astype(F32)
        delta = jnp.sum(product.T, axis=0, keepdims=True)
        both = jnp.concatenate([lse_ref[pl.ds(head, 1), :], delta], axis=1)
        rows = three_parts(both) + [jnp.zeros((AUX - 3, 2 * DH), F32)]
        block[QR + KR :, :] = jnp.concatenate(rows, axis=0).astype(BF16)


def copy_kernel(source, out):
    out[...] = source[...]


def join_kernel(b2, b0, b1, b3, q_out, kv_out):
    aux = []
    for j, block in enumerate((b0, b1, b2, b3)):
        q_out[j * QR : (j + 1) * QR, :] = block[:QR, :]
        kv_out[j * KR : (j + 1) * KR, :] = block[QR : QR + KR, :]
        aux.append(block[QR + KR :, :].astype(F32)[:3])
    aux.append(jnp.zeros((AUX - 12, 2 * DH), F32))
    q_out[QS:, :] = jnp.concatenate(aux, axis=0).astype(BF16)


def load_queries(blocks, q_all, terms):
    for b, block in enumerate(blocks):
        q_all[b * QS : (b + 1) * QS, :] = block[:QS, :]
        aux = block[QS:, :].astype(F32)
        for j in range(4):
            total = aux[3 * j : 3 * j + 1] + aux[3 * j + 1 : 3 * j + 2] + aux[3 * j + 2 : 3 * j + 3]
            cols = slice(b * QS + j * QR, b * QS + (j + 1) * QR)
            terms[0:1, cols] = total[:, :DH] * LOG2E
            terms[1:2, cols] = total[:, DH:]


def tile_terms(q_all, kv, terms, p_all, ds_all):
    for first in range(0, 2 * QS, QS):
        cols = slice(first, first + QS)
        q, g = q_all[cols, :DH], q_all[cols, DH:]
        s = lax.dot_general(kv[:, :DH], q, NT, preferred_element_type=F32)
        p = jnp.exp2(s * (FACTOR * LOG2E) - terms[0:1, cols])
        dp = lax.dot_general(kv[:, DH:], g, NT, preferred_element_type=F32)
        p_all[:, cols] = p.astype(BF16)
        ds_all[:, cols] = (p * (dp - terms[1:2, cols]) * FACTOR).astype(BF16)
    dv = jnp.dot(p_all[...], q_all[:, DH:], preferred_element_type=F32)
    dk = jnp.dot(ds_all[...], q_all[:, :DH], preferred_element_type=F32)
    dq = jnp.dot(kv[:, :DH].T, ds_all[...], preferred_element_type=F32)
    return dk, dv, dq


def attend_kernel(tiles, old_q, old_kv, *refs):
    refs = list(refs)
    pieces = [refs.pop(0) for _ in range(2 * tiles)]
    blocks = [refs.pop(0) for _ in range(2)]
    dq_old = refs.pop(0) if old_q else None
    dkv_old = [refs.pop(0) for _ in range(tiles)] if old_kv else None
    dkv_out = [refs.pop(0) for _ in range(tiles)]
    q_all, kv, terms, p_all, ds_all = refs[-5:]
    dq_out = refs[:-5]
    load_queries(blocks, q_all, terms)
    total = dq_old[...] if old_q else None
    for i in range(tiles):
        kv[i, :KS, :] = pieces[2 * i][...]
        kv[i, KS:, :] = pieces[2 * i + 1][...]
        dk, dv, dq = tile_terms(q_all, kv.at[i], terms, p_all, ds_all)
        if old_kv:
            dk = dk + dkv_old[i][:, :DH]
            dv = dv + dkv_old[i][:, DH:]
        dkv_out[i][:, :DH] = dk.astype(dkv_out[i].dtype)
        dkv_out[i][:, DH:] = dv.astype(dkv_out[i].dtype)
        total = dq if total is None else total + dq
    if len(dq_out) == 1:
        dq_out[0][...] = total
    else:
        for b, out in enumerate(dq_out):
            out[...] = total[:, b * QS : (b + 1) * QS].T.astype(out.dtype)


def add_kernel(a, b, out):
    out[...] = (a[...].astype(F32) + b[...].astype(F32)).astype(out.dtype)


def split_kernel(*refs):
    own, passed = refs[-2:]
    half = own.shape[0]
    for rows, out in ((slice(0, half), own), (slice(half, 2 * half), passed)):
        total = refs[0][rows, :]
        for ref in refs[1:-2]:
            total = total + ref[rows, :].astype(F32)
        out[...] = total.astype(out.dtype)


def chip_sum_kernel(q23, q0, k0, q1, k1, *outs):
    dq = q0[...] + q1[...].astype(F32) + q23[...]
    dkv = k0[...] + k1[...].astype(F32)
    for j, out in enumerate(outs):
        part = dq[j * QR : (j + 1) * QR]
        wide = jnp.concatenate([part[: QR // 2], part[QR // 2 :]], axis=1)
        out[:KR, :] = wide.astype(out.dtype)
        out[KR:, :] = dkv[j * KR : (j + 1) * KR].astype(out.dtype)


def unpack_kernel(b2, b0, b1, b3, dq, dk, dv):
    y = lax.axis_index("row") % 4
    for j, block in enumerate((b0, b1, b2, b3)):
        cols = pl.ds(pl.multiple_of(lax.rem(y + j, 4) * DH, DH), DH)
        dq[: QR // 2, cols] = block[:KR, :DH].astype(F32)
        dq[QR // 2 :, cols] = block[:KR, DH:].astype(F32)
        dk[:, cols] = block[KR:, :DH].astype(F32)
        dv[:, cols] = block[KR:, DH:].astype(F32)


def call(kernel, outs, args, scratch=(), flops=0, space=VMEM, limit=40):
    total = sum(a.size * a.dtype.itemsize for a in args) + sum(
        math.prod(shape) * jnp.dtype(kind).itemsize for shape, kind in outs
    )
    return pl.pallas_call(
        kernel,
        out_shape=[jax.ShapeDtypeStruct(shape, kind) for shape, kind in outs],
        in_specs=[space] * len(args),
        out_specs=[VMEM] * len(outs),
        scratch_shapes=list(scratch),
        compiler_params=pltpu.CompilerParams(vmem_limit_bytes=limit * 1024 * 1024),
        cost_estimate=pl.CostEstimate(flops=flops, bytes_accessed=total, transcendentals=0),
    )(*args)


def attend(blocks, tiles, dq_old, dkv_old, dq_out, dkv_out):
    args = [piece for tile in tiles for piece in tile] + [*blocks]
    args += ([] if dq_old is None else [dq_old]) + list(dkv_old or ())
    rows = 2 * QS
    outs = call(
        functools.partial(attend_kernel, len(tiles), dq_old is not None, dkv_old is not None),
        [((TILE, 2 * DH), kind) for kind in dkv_out] + dq_out,
        args,
        scratch=[
            pltpu.VMEM((rows, 2 * DH), BF16),
            pltpu.VMEM((len(tiles), TILE, 2 * DH), BF16),
            pltpu.VMEM((8, rows), F32),
            pltpu.VMEM((TILE, rows), BF16),
            pltpu.VMEM((TILE, rows), BF16),
        ],
        flops=10 * rows * TILE * len(tiles) * DH,
    )
    return outs[len(tiles) :], outs[: len(tiles)]


def per_device(queries, keys, values, outputs, d_out, lse):
    args = (queries, keys, values, outputs, d_out, lse)
    with jax.named_scope("pack"):
        scratch = [pltpu.VMEM(a.shape, a.dtype) for a in args] + [pltpu.SemaphoreType.DMA((6,))]
        place = pl.BlockSpec(memory_space=pltpu.HBM)
        far, plus, minus = call(
            functools.partial(pack_kernel, (2, 1, 3)),
            [((BLK, 2 * DH), BF16)] * 3,
            args,
            scratch=scratch,
            space=place,
            limit=56,
        )
        here = call(
            functools.partial(pack_kernel, (0,)),
            [((BLK, 2 * DH), BF16)],
            args,
            scratch=scratch,
            space=place,
            limit=56,
        )[0]
        here = call(copy_kernel, [((BLK, 2 * DH), BF16)], (here,))[0]
    with jax.named_scope("heads_over_y"):
        blocks = [along_y(far, 2), here, along_y(plus, 1), along_y(minus, 3)]
    with jax.named_scope("join"):
        q, kv = call(join_kernel, [((QS + AUX, 2 * DH), BF16), ((KS, 2 * DH), BF16)], blocks)
    with jax.named_scope("queries_over_x"):
        q1 = swap_x(q, 0)
        q2 = swap_x(q, 1)
        q3 = swap_x(q1, 1)
    with jax.named_scope("keys_over_z"):
        near = [(kv, swap_z(kv, 0)), (swap_z(kv, 1), swap_z(kv, 2))]
        k_a, k_b = near
        o_a, o_b = [tuple(other_core(piece) for piece in pair) for pair in near]
    sums = [((DH, 2 * QS), F32)]
    q_a = (q, q1)
    q2, k_b = lax.optimization_barrier((q2, k_b))
    with jax.named_scope("attend_a_b"):
        (dq_a,), (dkv_b,) = attend(q_a, (k_b,), None, None, sums, (F32,))
        (dq_a,), (dko_b,) = attend(q_a, (o_b,), dq_a, None, sums, (F32,))
    with jax.named_scope("attend_a_a_other"):
        (dq_a,), (dko_a,) = attend(q_a, (o_a,), dq_a, None, sums, (F32,))
    q3, dq_a = lax.optimization_barrier((q3, dq_a))
    q_b = (q2, q3)
    with jax.named_scope("attend_b_b"):
        (dq_b,), (dko_b, dkv_b) = attend(q_b, (o_b, k_b), None, (dko_b, dkv_b), sums, (BF16, F32))
    with jax.named_scope("sum_keys_over_core"):
        sent_b = call(add_kernel, [((TILE, 2 * DH), BF16)], (dkv_b, other_core(dko_b)))[0]
    with jax.named_scope("attend_b_a_other"):
        (dq_b,), (dko_a,) = attend(q_b, (o_a,), dq_b, (dko_a,), sums, (BF16,))
    dq_b, sent_b = lax.optimization_barrier((dq_b, sent_b))
    with jax.named_scope("attend_b_a"):
        (dq2, dq3), (dkv_a,) = attend(q_b, (k_a,), dq_b, None, [((QS, DH), BF16)] * 2, (F32,))
    with jax.named_scope("sum_queries_over_x"):
        got2, got3 = swap_x(dq2, 1), swap_x(dq3, 2)
    with jax.named_scope("sum_keys_over_z"):
        got_b = swap_z(sent_b, 1)
    with jax.named_scope("sum_keys_over_core"):
        got_other = other_core(dko_a)
    with jax.named_scope("attend_a_a"):
        (dq0, dq1), (dkv_own,) = attend(
            q_a, (k_a,), dq_a, (dkv_a,), [((QS, DH), F32), ((QS, DH), BF16)], (F32,)
        )
    with jax.named_scope("sum_queries_over_x"):
        got1 = swap_x(dq1, 0)
        got23 = call(add_kernel, [((QS, DH), F32)], (got2, got3), flops=4 * 10**9)[0]
    with jax.named_scope("sum_keys_over_z"):
        k_own, k_sent = call(
            split_kernel, [((KS, 2 * DH), F32), ((KS, 2 * DH), BF16)], (dkv_own, got_other, got_b)
        )
        k_got = swap_z(k_sent, 0)
    with jax.named_scope("chip_sum"):
        backs = call(
            chip_sum_kernel,
            [((2 * KR, 2 * DH), F32)] + [((2 * KR, 2 * DH), BF16)] * 3,
            (got23, dq0, k_own, got1, k_got),
        )
    with jax.named_scope("back_over_y"):
        far = along_y(backs[2], 2)
        backs = [far, backs[0], along_y(backs[1], 3), along_y(backs[3], 1)]
    with jax.named_scope("unpack"):
        return tuple(
            call(
                unpack_kernel,
                [((QR, H * DH), F32), ((KR, H * DH), F32), ((KR, H * DH), F32)],
                backs,
            )
        )


def solution(mesh):
    return jax.shard_map(
        per_device,
        mesh=mesh,
        in_specs=(
            P(("row", "col"), None),
            P(("col", "row"), None),
            P(("col", "row"), None),
            P(("row", "col"), None),
            P(("row", "col"), None),
            P(None, ("row", "col")),
        ),
        out_specs=(P(("row", "col"), None), P(("col", "row"), None), P(("col", "row"), None)),
        check_vma=False,
    )
```

```python
import functools
import math

import jax
import jax.numpy as jnp
from jax import lax
from jax.experimental import pallas as pl
from jax.experimental.pallas import tpu as pltpu
from jax.sharding import PartitionSpec as P

H = 4
DH = 128
AXES = ("row", "col")
F32 = jnp.float32
BF16 = jnp.bfloat16
QR = 128
KR = 64
AUX = 16
TILE = 512
HINT = 1.0
LATE = 4 * 10**9
BLK = QR + KR + AUX
QS = 4 * QR
KS = 4 * KR
FACTOR = 1.0 / math.sqrt(DH)
LOG2E = math.log2(math.e)
VMEM = pl.BlockSpec(memory_space=pltpu.VMEM)
NT = (((1,), (1,)), ((), ()))


def linear(x, y, z, c):
    return ((z % 2) * 4 + y) * 16 + (z // 2) * 8 + x * 2 + c


def move(value, target):
    pairs = []
    for x in range(4):
        for y in range(4):
            for z in range(4):
                for c in range(2):
                    pairs.append((linear(x, y, z, c), linear(*target(x, y, z, c))))
    return lax.ppermute(value, AXES, pairs)


def other_core(value):
    return move(value, lambda x, y, z, c: (x, y, z, 1 - c))


def partner(place, core, kind):
    if kind == 2:
        return (place + 2) % 4
    up = place % 2 == (kind + core) % 2
    return (place + (1 if up else -1)) % 4


def swap_y(value, kind):
    return move(value, lambda x, y, z, c: (x, partner(y, c, kind), z, c))


def swap_x(value, kind):
    return move(value, lambda x, y, z, c: (partner(x, c, kind), y, z, c))


def swap_z(value, kind):
    return move(value, lambda x, y, z, c: (x, y, partner(z, c, kind), c))


def three_parts(value):
    high = value.astype(BF16).astype(F32)
    rest = value - high
    middle = rest.astype(BF16).astype(F32)
    return [high, middle, rest - middle]


def head_of(kind):
    y = lax.axis_index("row") % 4
    if kind is None:
        return y
    if kind == 2:
        return lax.rem(y + 2, 4)
    odd = lax.rem(y + kind + lax.axis_index("col"), 2)
    return lax.rem(y + 1 + 2 * odd, 4)


def pack_kernel(kinds, *refs):
    blocks, bufs, sem = refs[6:-7], refs[-7:-1], refs[-1]
    copies = [pltpu.make_async_copy(refs[i], bufs[i], sem.at[i]) for i in range(6)]
    for copy in copies:
        copy.start()
    for copy in copies:
        copy.wait()
    q_ref, k_ref, v_ref, o_ref, g_ref, lse_ref = bufs
    for kind, block in zip(kinds, blocks):
        head = head_of(kind)
        cols = pl.ds(pl.multiple_of(head * DH, DH), DH)
        g = g_ref[:, cols]
        block[:QR, :DH] = q_ref[:, cols]
        block[:QR, DH:] = g
        block[QR : QR + KR, :DH] = k_ref[:, cols]
        block[QR : QR + KR, DH:] = v_ref[:, cols]
        product = g.astype(F32) * o_ref[:, cols].astype(F32)
        delta = jnp.sum(product.T, axis=0, keepdims=True)
        both = jnp.concatenate([lse_ref[pl.ds(head, 1), :], delta], axis=1)
        rows = three_parts(both) + [jnp.zeros((AUX - 3, 2 * DH), F32)]
        block[QR + KR :, :] = jnp.concatenate(rows, axis=0).astype(BF16)


def copy_kernel(source, out):
    out[...] = source[...]


def join_kernel(b0, b1, b3, b2, q_out, kv_out):
    aux = []
    for j, block in enumerate((b0, b1, b2, b3)):
        q_out[j * QR : (j + 1) * QR, :] = block[:QR, :]
        kv_out[j * KR : (j + 1) * KR, :] = block[QR : QR + KR, :]
        aux.append(block[QR + KR :, :].astype(F32)[:3])
    aux.append(jnp.zeros((AUX - 12, 2 * DH), F32))
    q_out[QS:, :] = jnp.concatenate(aux, axis=0).astype(BF16)


def load_queries(blocks, q_all, terms):
    for b, block in enumerate(blocks):
        q_all[b * QS : (b + 1) * QS, :] = block[:QS, :]
        aux = block[QS:, :].astype(F32)
        for j in range(4):
            total = aux[3 * j : 3 * j + 1] + aux[3 * j + 1 : 3 * j + 2] + aux[3 * j + 2 : 3 * j + 3]
            cols = slice(b * QS + j * QR, b * QS + (j + 1) * QR)
            terms[0:1, cols] = total[:, :DH] * LOG2E
            terms[1:2, cols] = total[:, DH:]


def tile_terms(q_all, kv, terms, p_all, ds_all):
    q, g = q_all[:, :DH], q_all[:, DH:]
    s = lax.dot_general(kv[:, :DH], q, NT, preferred_element_type=F32)
    p = jnp.exp2(s * (FACTOR * LOG2E) - terms[0:1, :])
    dp = lax.dot_general(kv[:, DH:], g, NT, preferred_element_type=F32)
    p_all[...] = p.astype(BF16)
    ds_all[...] = (p * (dp - terms[1:2, :]) * FACTOR).astype(BF16)
    dv = jnp.dot(p_all[...], g, preferred_element_type=F32)
    dk = jnp.dot(ds_all[...], q, preferred_element_type=F32)
    dq = jnp.dot(kv[:, :DH].T, ds_all[...], preferred_element_type=F32)
    return dk, dv, dq


def attend_kernel(tiles, old_q, old_kv, *refs):
    refs = list(refs)
    pieces = [refs.pop(0) for _ in range(2 * tiles)]
    blocks = [refs.pop(0) for _ in range(2)]
    dq_old = refs.pop(0) if old_q else None
    dkv_old = [refs.pop(0) for _ in range(tiles)] if old_kv else None
    dkv_out = [refs.pop(0) for _ in range(tiles)]
    q_all, kv, terms, p_all, ds_all = refs[-5:]
    dq_out = refs[:-5]
    load_queries(blocks, q_all, terms)
    total = dq_old[...] if old_q else None
    for i in range(tiles):
        kv[i, :KS, :] = pieces[2 * i][...]
        kv[i, KS:, :] = pieces[2 * i + 1][...]
        dk, dv, dq = tile_terms(q_all, kv.at[i], terms, p_all, ds_all)
        if old_kv:
            dk = dk + dkv_old[i][:, :DH]
            dv = dv + dkv_old[i][:, DH:]
        dkv_out[i][:, :DH] = dk.astype(dkv_out[i].dtype)
        dkv_out[i][:, DH:] = dv.astype(dkv_out[i].dtype)
        total = dq if total is None else total + dq
    if len(dq_out) == 1:
        dq_out[0][...] = total
    else:
        for b, out in enumerate(dq_out):
            out[...] = total[:, b * QS : (b + 1) * QS].T.astype(out.dtype)


def add_kernel(a, b, out):
    out[...] = (a[...].astype(F32) + b[...].astype(F32)).astype(out.dtype)


def split_kernel(*refs):
    own, passed = refs[-2:]
    half = own.shape[0]
    for rows, out in ((slice(0, half), own), (slice(half, 2 * half), passed)):
        total = refs[0][rows, :]
        for ref in refs[1:-2]:
            total = total + ref[rows, :].astype(F32)
        out[...] = total.astype(out.dtype)


def chip_sum_kernel(q23, q0, k0, k1, q1, *outs):
    dq = q0[...] + q1[...].astype(F32) + q23[...]
    dkv = k0[...] + k1[...].astype(F32)
    for j, out in enumerate(outs):
        part = dq[j * QR : (j + 1) * QR]
        wide = jnp.concatenate([part[: QR // 2], part[QR // 2 :]], axis=1)
        out[:KR, :] = wide.astype(out.dtype)
        out[KR:, :] = dkv[j * KR : (j + 1) * KR].astype(out.dtype)


def unpack_kernel(b0, b1, b3, b2, dq, dk, dv):
    for kind, block in ((None, b0), (0, b1), (2, b2), (1, b3)):
        cols = pl.ds(pl.multiple_of(head_of(kind) * DH, DH), DH)
        dq[: QR // 2, cols] = block[:KR, :DH].astype(F32)
        dq[QR // 2 :, cols] = block[:KR, DH:].astype(F32)
        dk[:, cols] = block[KR:, :DH].astype(F32)
        dv[:, cols] = block[KR:, DH:].astype(F32)


def call(kernel, outs, args, scratch=(), flops=0, space=VMEM, limit=40):
    total = sum(a.size * a.dtype.itemsize for a in args) + sum(
        math.prod(shape) * jnp.dtype(kind).itemsize for shape, kind in outs
    )
    return pl.pallas_call(
        kernel,
        out_shape=[jax.ShapeDtypeStruct(shape, kind) for shape, kind in outs],
        in_specs=[space] * len(args),
        out_specs=[VMEM] * len(outs),
        scratch_shapes=list(scratch),
        compiler_params=pltpu.CompilerParams(vmem_limit_bytes=limit * 1024 * 1024),
        cost_estimate=pl.CostEstimate(flops=flops, bytes_accessed=total, transcendentals=0),
    )(*args)


def attend(blocks, tiles, dq_old, dkv_old, dq_out, dkv_out):
    args = [piece for tile in tiles for piece in tile] + [*blocks]
    args += ([] if dq_old is None else [dq_old]) + list(dkv_old or ())
    rows = 2 * QS
    outs = call(
        functools.partial(attend_kernel, len(tiles), dq_old is not None, dkv_old is not None),
        [((TILE, 2 * DH), kind) for kind in dkv_out] + dq_out,
        args,
        scratch=[
            pltpu.VMEM((rows, 2 * DH), BF16),
            pltpu.VMEM((len(tiles), TILE, 2 * DH), BF16),
            pltpu.VMEM((8, rows), F32),
            pltpu.VMEM((TILE, rows), BF16),
            pltpu.VMEM((TILE, rows), BF16),
        ],
        flops=int(10 * rows * TILE * len(tiles) * DH * HINT),
    )
    return outs[len(tiles) :], outs[: len(tiles)]


def per_device(queries, keys, values, outputs, d_out, lse):
    args = (queries, keys, values, outputs, d_out, lse)
    with jax.named_scope("pack"):
        scratch = [pltpu.VMEM(a.shape, a.dtype) for a in args] + [pltpu.SemaphoreType.DMA((6,))]
        place = pl.BlockSpec(memory_space=pltpu.HBM)
        far, first, second = call(
            functools.partial(pack_kernel, (2, 0, 1)),
            [((BLK, 2 * DH), BF16)] * 3,
            args,
            scratch=scratch,
            space=place,
            limit=56,
        )
        here = call(
            functools.partial(pack_kernel, (None,)),
            [((BLK, 2 * DH), BF16)],
            args,
            scratch=scratch,
            space=place,
            limit=56,
        )[0]
        here = call(copy_kernel, [((BLK, 2 * DH), BF16)], (here,))[0]
    with jax.named_scope("heads_over_y"):
        blocks = [here, swap_y(first, 0), swap_y(second, 1), swap_y(far, 2)]
    with jax.named_scope("join"):
        q, kv = call(join_kernel, [((QS + AUX, 2 * DH), BF16), ((KS, 2 * DH), BF16)], blocks)
    with jax.named_scope("queries_over_x"):
        q1 = swap_x(q, 0)
        q2 = swap_x(q, 1)
        q3 = swap_x(q1, 1)
    with jax.named_scope("keys_over_z"):
        near = [(kv, swap_z(kv, 0)), (swap_z(kv, 1), swap_z(kv, 2))]
        k_a, k_b = near
        o_a, o_b = [tuple(other_core(piece) for piece in pair) for pair in near]
    sums = [((DH, 2 * QS), F32)]
    q_a = (q, q1)
    q2, k_b = lax.optimization_barrier((q2, k_b))
    with jax.named_scope("attend_a_b"):
        (dq_a,), (dkv_b,) = attend(q_a, (k_b,), None, None, sums, (F32,))
        (dq_a,), (dko_b,) = attend(q_a, (o_b,), dq_a, None, sums, (F32,))
    with jax.named_scope("attend_a_a_other"):
        (dq_a,), (dko_a,) = attend(q_a, (o_a,), dq_a, None, sums, (F32,))
    q3, dq_a = lax.optimization_barrier((q3, dq_a))
    q_b = (q2, q3)
    with jax.named_scope("attend_b_b"):
        (dq_b,), (dko_b, dkv_b) = attend(q_b, (o_b, k_b), None, (dko_b, dkv_b), sums, (BF16, F32))
    with jax.named_scope("sum_keys_over_core"):
        sent_b = call(add_kernel, [((TILE, 2 * DH), BF16)], (dkv_b, other_core(dko_b)))[0]
    with jax.named_scope("attend_b_a_other"):
        (dq_b,), (dko_a,) = attend(q_b, (o_a,), dq_b, (dko_a,), sums, (BF16,))
    dq_b, sent_b = lax.optimization_barrier((dq_b, sent_b))
    with jax.named_scope("attend_b_a"):
        (dq2, dq3), (dkv_a,) = attend(q_b, (k_a,), dq_b, None, [((QS, DH), BF16)] * 2, (F32,))
    with jax.named_scope("sum_queries_over_x"):
        got2, got3 = swap_x(dq2, 1), swap_x(dq3, 2)
    with jax.named_scope("sum_keys_over_z"):
        got_b = swap_z(sent_b, 1)
    with jax.named_scope("sum_keys_over_core"):
        got_other = other_core(dko_a)
    with jax.named_scope("attend_a_a"):
        (dq0, dq1), (dkv_own,) = attend(
            q_a, (k_a,), dq_a, (dkv_a,), [((QS, DH), F32), ((QS, DH), BF16)], (F32,)
        )
    with jax.named_scope("sum_queries_over_x"):
        got1 = swap_x(dq1, 0)
        got23 = call(add_kernel, [((QS, DH), F32)], (got2, got3), flops=LATE)[0]
    with jax.named_scope("sum_keys_over_z"):
        k_own, k_sent = call(
            split_kernel, [((KS, 2 * DH), F32), ((KS, 2 * DH), BF16)], (dkv_own, got_other, got_b)
        )
        k_got = swap_z(k_sent, 0)
    with jax.named_scope("chip_sum"):
        backs = call(
            chip_sum_kernel,
            [((2 * KR, 2 * DH), F32)] + [((2 * KR, 2 * DH), BF16)] * 3,
            (got23, dq0, k_own, k_got, got1),
        )
    with jax.named_scope("back_over_y"):
        far = swap_y(backs[2], 2)
        backs = [backs[0], swap_y(backs[1], 0), swap_y(backs[3], 1), far]
    with jax.named_scope("unpack"):
        return tuple(
            call(
                unpack_kernel,
                [((QR, H * DH), F32), ((KR, H * DH), F32), ((KR, H * DH), F32)],
                backs,
            )
        )


def solution(mesh):
    return jax.shard_map(
        per_device,
        mesh=mesh,
        in_specs=(
            P(("row", "col"), None),
            P(("col", "row"), None),
            P(("col", "row"), None),
            P(("row", "col"), None),
            P(("row", "col"), None),
            P(None, ("row", "col")),
        ),
        out_specs=(P(("row", "col"), None), P(("col", "row"), None), P(("col", "row"), None)),
        check_vma=False,
    )
```

```python
import functools
import math

import jax
import jax.numpy as jnp
from jax import lax
from jax.experimental import pallas as pl
from jax.experimental.pallas import tpu as pltpu
from jax.sharding import PartitionSpec as P

H = 4
DH = 128
AXES = ("row", "col")
F32 = jnp.float32
BF16 = jnp.bfloat16
QR = 128
KR = 64
AUX = 16
TILE = 512
HINT = 1.0
LATE = 4 * 10**9
BLK = QR + KR + AUX
QS = 4 * QR
KS = 4 * KR
FACTOR = 1.0 / math.sqrt(DH)
LOG2E = math.log2(math.e)
VMEM = pl.BlockSpec(memory_space=pltpu.VMEM)
HBM = pl.BlockSpec(memory_space=pltpu.HBM)
NT = (((1,), (1,)), ((), ()))


def linear(x, y, z, c):
    return ((z % 2) * 4 + y) * 16 + (z // 2) * 8 + x * 2 + c


def move(value, target):
    pairs = []
    for x in range(4):
        for y in range(4):
            for z in range(4):
                for c in range(2):
                    pairs.append((linear(x, y, z, c), linear(*target(x, y, z, c))))
    return lax.ppermute(value, AXES, pairs)


def other_core(value):
    return move(value, lambda x, y, z, c: (x, y, z, 1 - c))


def partner(place, core, kind):
    if kind == 2:
        return (place + 2) % 4
    up = place % 2 == (kind + core) % 2
    return (place + (1 if up else -1)) % 4


def swap_heads(value, kind):
    return move(value, lambda x, y, z, c: (x, partner(y, c, kind), z, c))


def swap_queries(value, kind):
    return move(value, lambda x, y, z, c: (x, y, partner(z, c, kind), c))


def swap_keys(value, kind):
    return move(value, lambda x, y, z, c: (partner(x, c, kind), y, z, c))


def three_parts(value):
    high = value.astype(BF16).astype(F32)
    rest = value - high
    middle = rest.astype(BF16).astype(F32)
    return [high, middle, rest - middle]


def head_of(kind):
    y = lax.axis_index("row") % 4
    if kind is None:
        return y
    if kind == 2:
        return lax.rem(y + 2, 4)
    odd = lax.rem(y + kind + lax.axis_index("col"), 2)
    return lax.rem(y + 1 + 2 * odd, 4)


def pack_kernel(kinds, *refs):
    count = len(kinds)
    sources, blocks = refs[:6], refs[6 : 6 + count]
    bufs, built, in_sem, out_sem = refs[6 + count : 12 + count], *refs[12 + count :]
    loads = [
        pltpu.make_async_copy(source, buf, in_sem.at[i])
        for i, (source, buf) in enumerate(zip(sources, bufs))
    ]
    for copy in loads:
        copy.start()
    q_buf, k_buf, v_buf, g_buf, o_buf, lse_buf = bufs
    heads = [head_of(kind) for kind in kinds]
    columns = [pl.ds(pl.multiple_of(head * DH, DH), DH) for head in heads]
    sends = []

    def send(j, part, first, rows):
        copy = pltpu.make_async_copy(
            built.at[j, pl.ds(first, rows), :],
            blocks[j].at[pl.ds(first, rows), :],
            out_sem.at[2 * j + part],
        )
        copy.start()
        sends.append(copy)

    for copy in loads[:4]:
        copy.wait()
    for j, cols in enumerate(columns):
        built[j, :QR, :DH] = q_buf[:, cols]
        built[j, :QR, DH:] = g_buf[:, cols]
        built[j, QR : QR + KR, :DH] = k_buf[:, cols]
        built[j, QR : QR + KR, DH:] = v_buf[:, cols]
        send(j, 0, 0, QR + KR)
    for copy in loads[4:]:
        copy.wait()
    for j, (head, cols) in enumerate(zip(heads, columns)):
        product = g_buf[:, cols].astype(F32) * o_buf[:, cols].astype(F32)
        delta = jnp.sum(product.T, axis=0, keepdims=True)
        both = jnp.concatenate([lse_buf[pl.ds(head, 1), :], delta], axis=1)
        rows = three_parts(both) + [jnp.zeros((AUX - 3, 2 * DH), F32)]
        built[j, QR + KR :, :] = jnp.concatenate(rows, axis=0).astype(BF16)
        send(j, 1, QR + KR, AUX)
    for copy in sends:
        copy.wait()


def copy_kernel(source, out):
    out[...] = source[...]


def join_kernel(b2, b0, b1, b3, q_out, kv_out):
    aux = []
    for j, block in enumerate((b0, b1, b2, b3)):
        q_out[j * QR : (j + 1) * QR, :] = block[:QR, :]
        kv_out[j * KR : (j + 1) * KR, :] = block[QR : QR + KR, :]
        aux.append(block[QR + KR :, :].astype(F32)[:3])
    aux.append(jnp.zeros((AUX - 12, 2 * DH), F32))
    q_out[QS:, :] = jnp.concatenate(aux, axis=0).astype(BF16)


def load_queries(blocks, q_all, terms):
    for b, block in enumerate(blocks):
        q_all[b * QS : (b + 1) * QS, :] = block[:QS, :]
        aux = block[QS:, :].astype(F32)
        for j in range(4):
            total = aux[3 * j : 3 * j + 1] + aux[3 * j + 1 : 3 * j + 2] + aux[3 * j + 2 : 3 * j + 3]
            cols = slice(b * QS + j * QR, b * QS + (j + 1) * QR)
            terms[0:1, cols] = total[:, :DH] * LOG2E
            terms[1:2, cols] = total[:, DH:]


def tile_terms(q_all, kv, terms, p_all, ds_all):
    q, g = q_all[:, :DH], q_all[:, DH:]
    s = lax.dot_general(kv[:, :DH], q, NT, preferred_element_type=F32)
    p = jnp.exp2(s * (FACTOR * LOG2E) - terms[0:1, :])
    dp = lax.dot_general(kv[:, DH:], g, NT, preferred_element_type=F32)
    p_all[...] = p.astype(BF16)
    ds_all[...] = (p * (dp - terms[1:2, :]) * FACTOR).astype(BF16)
    dv = jnp.dot(p_all[...], g, preferred_element_type=F32)
    dk = jnp.dot(ds_all[...], q, preferred_element_type=F32)
    dq = jnp.dot(kv[:, :DH].T, ds_all[...], preferred_element_type=F32)
    return dk, dv, dq


def attend_kernel(tiles, old_q, old_kv, *refs):
    refs = list(refs)
    pieces = [refs.pop(0) for _ in range(2 * tiles)]
    blocks = [refs.pop(0) for _ in range(2)]
    dq_old = refs.pop(0) if old_q else None
    dkv_old = [refs.pop(0) for _ in range(tiles)] if old_kv else None
    dkv_out = [refs.pop(0) for _ in range(tiles)]
    q_all, kv, terms, p_all, ds_all = refs[-5:]
    dq_out = refs[:-5]
    load_queries(blocks, q_all, terms)
    total = dq_old[...] if old_q else None
    for i in range(tiles):
        kv[i, :KS, :] = pieces[2 * i][...]
        kv[i, KS:, :] = pieces[2 * i + 1][...]
        dk, dv, dq = tile_terms(q_all, kv.at[i], terms, p_all, ds_all)
        if old_kv:
            dk = dk + dkv_old[i][:, :DH]
            dv = dv + dkv_old[i][:, DH:]
        dkv_out[i][:, :DH] = dk.astype(dkv_out[i].dtype)
        dkv_out[i][:, DH:] = dv.astype(dkv_out[i].dtype)
        total = dq if total is None else total + dq
    if len(dq_out) == 1:
        dq_out[0][...] = total
    else:
        for b, out in enumerate(dq_out):
            out[...] = total[:, b * QS : (b + 1) * QS].T.astype(out.dtype)


def add_kernel(a, b, out):
    out[...] = (a[...].astype(F32) + b[...].astype(F32)).astype(out.dtype)


def split_kernel(*refs):
    own, passed = refs[-2:]
    half = own.shape[0]
    for rows, out in ((slice(0, half), own), (slice(half, 2 * half), passed)):
        total = refs[0][rows, :]
        for ref in refs[1:-2]:
            total = total + ref[rows, :].astype(F32)
        out[...] = total.astype(out.dtype)


def chip_sum_kernel(q23, q0, k0, k1, q1, *outs):
    dq = q0[...] + q1[...].astype(F32) + q23[...]
    dkv = k0[...] + k1[...].astype(F32)
    for j, out in enumerate(outs):
        part = dq[j * QR : (j + 1) * QR]
        wide = jnp.concatenate([part[: QR // 2], part[QR // 2 :]], axis=1)
        out[:KR, :] = wide.astype(out.dtype)
        out[KR:, :] = dkv[j * KR : (j + 1) * KR].astype(out.dtype)


def unpack_kernel(b0, b1, b3, b2, dq, dk, dv):
    for kind, block in ((None, b0), (0, b1), (2, b2), (1, b3)):
        cols = pl.ds(pl.multiple_of(head_of(kind) * DH, DH), DH)
        dq[: QR // 2, cols] = block[:KR, :DH].astype(F32)
        dq[QR // 2 :, cols] = block[:KR, DH:].astype(F32)
        dk[:, cols] = block[KR:, :DH].astype(F32)
        dv[:, cols] = block[KR:, DH:].astype(F32)


def call(kernel, outs, args, scratch=(), flops=0, space=VMEM, out_space=VMEM, limit=40):
    total = sum(a.size * a.dtype.itemsize for a in args) + sum(
        math.prod(shape) * jnp.dtype(kind).itemsize for shape, kind in outs
    )
    return pl.pallas_call(
        kernel,
        out_shape=[jax.ShapeDtypeStruct(shape, kind) for shape, kind in outs],
        in_specs=[space] * len(args),
        out_specs=[out_space] * len(outs),
        scratch_shapes=list(scratch),
        compiler_params=pltpu.CompilerParams(vmem_limit_bytes=limit * 1024 * 1024),
        cost_estimate=pl.CostEstimate(flops=flops, bytes_accessed=total, transcendentals=0),
    )(*args)


def attend(blocks, tiles, dq_old, dkv_old, dq_out, dkv_out):
    args = [piece for tile in tiles for piece in tile] + [*blocks]
    args += ([] if dq_old is None else [dq_old]) + list(dkv_old or ())
    rows = 2 * QS
    outs = call(
        functools.partial(attend_kernel, len(tiles), dq_old is not None, dkv_old is not None),
        [((TILE, 2 * DH), kind) for kind in dkv_out] + dq_out,
        args,
        scratch=[
            pltpu.VMEM((rows, 2 * DH), BF16),
            pltpu.VMEM((len(tiles), TILE, 2 * DH), BF16),
            pltpu.VMEM((8, rows), F32),
            pltpu.VMEM((TILE, rows), BF16),
            pltpu.VMEM((TILE, rows), BF16),
        ],
        flops=int(10 * rows * TILE * len(tiles) * DH * HINT),
    )
    return outs[len(tiles) :], outs[: len(tiles)]


def per_device(queries, keys, values, outputs, d_out, lse):
    args = (queries, keys, values, d_out, outputs, lse)
    with jax.named_scope("pack"):
        def pack(kinds):
            count = len(kinds)
            return call(
                functools.partial(pack_kernel, kinds),
                [((BLK, 2 * DH), BF16)] * count,
                args,
                scratch=[pltpu.VMEM(a.shape, a.dtype) for a in args]
                + [
                    pltpu.VMEM((count, BLK, 2 * DH), BF16),
                    pltpu.SemaphoreType.DMA((6,)),
                    pltpu.SemaphoreType.DMA((2 * count,)),
                ],
                space=HBM,
                out_space=HBM,
                limit=56,
            )

        far, first, second = pack((2, 0, 1))
        here = pack((None,))[0]
        here = call(copy_kernel, [((BLK, 2 * DH), BF16)], (here,))[0]
    with jax.named_scope("heads_to_chips"):
        blocks = [swap_heads(far, 2), here, swap_heads(first, 0), swap_heads(second, 1)]
    with jax.named_scope("join"):
        q, kv = call(join_kernel, [((QS + AUX, 2 * DH), BF16), ((KS, 2 * DH), BF16)], blocks)
    with jax.named_scope("gather_queries"):
        q1 = swap_queries(q, 0)
        q2 = swap_queries(q, 1)
        q3 = swap_queries(q1, 1)
    with jax.named_scope("gather_keys"):
        near = [(kv, swap_keys(kv, 0)), (swap_keys(kv, 1), swap_keys(kv, 2))]
        k_a, k_b = near
        o_a, o_b = [tuple(other_core(piece) for piece in pair) for pair in near]
    sums = [((DH, 2 * QS), F32)]
    q_a = (q, q1)
    q2, k_b = lax.optimization_barrier((q2, k_b))
    with jax.named_scope("attend_a_b"):
        (dq_a,), (dkv_b,) = attend(q_a, (k_b,), None, None, sums, (F32,))
        (dq_a,), (dko_b, dko_a) = attend(q_a, (o_b, o_a), dq_a, None, sums, (F32,) * 2)
    q3, dq_a = lax.optimization_barrier((q3, dq_a))
    q_b = (q2, q3)
    with jax.named_scope("attend_b_b"):
        (dq_b,), (dko_b, dkv_b) = attend(q_b, (o_b, k_b), None, (dko_b, dkv_b), sums, (BF16, F32))
    with jax.named_scope("sum_keys_over_core"):
        sent_b = call(add_kernel, [((TILE, 2 * DH), BF16)], (dkv_b, other_core(dko_b)))[0]
    with jax.named_scope("attend_b_a_other"):
        (dq_b,), (dko_a,) = attend(q_b, (o_a,), dq_b, (dko_a,), sums, (BF16,))
    dq_b, sent_b = lax.optimization_barrier((dq_b, sent_b))
    with jax.named_scope("attend_b_a"):
        (dq2, dq3), (dkv_a,) = attend(q_b, (k_a,), dq_b, None, [((QS, DH), BF16)] * 2, (F32,))
    with jax.named_scope("sum_queries"):
        got2, got3 = swap_queries(dq2, 1), swap_queries(dq3, 2)
    with jax.named_scope("sum_keys"):
        got_b = swap_keys(sent_b, 1)
    with jax.named_scope("sum_keys_over_core"):
        got_other = other_core(dko_a)
    with jax.named_scope("attend_a_a"):
        (dq0, dq1), (dkv_own,) = attend(
            q_a, (k_a,), dq_a, (dkv_a,), [((QS, DH), F32), ((QS, DH), BF16)], (F32,)
        )
    with jax.named_scope("sum_queries"):
        got1 = swap_queries(dq1, 0)
        got23 = call(add_kernel, [((QS, DH), F32)], (got2, got3), flops=LATE)[0]
    with jax.named_scope("sum_keys"):
        k_own, k_sent = call(
            split_kernel, [((KS, 2 * DH), F32), ((KS, 2 * DH), BF16)], (dkv_own, got_other, got_b)
        )
        k_got = swap_keys(k_sent, 0)
    with jax.named_scope("chip_sum"):
        backs = call(
            chip_sum_kernel,
            [((2 * KR, 2 * DH), F32)] + [((2 * KR, 2 * DH), BF16)] * 3,
            (got23, dq0, k_own, k_got, got1),
        )
    with jax.named_scope("back_to_rows"):
        far = swap_heads(backs[2], 2)
        backs = [backs[0], swap_heads(backs[1], 0), swap_heads(backs[3], 1), far]
    with jax.named_scope("unpack"):
        return tuple(
            call(
                unpack_kernel,
                [((QR, H * DH), F32), ((KR, H * DH), F32), ((KR, H * DH), F32)],
                backs,
            )
        )


def solution(mesh):
    return jax.shard_map(
        per_device,
        mesh=mesh,
        in_specs=(
            P(("row", "col"), None),
            P(("col", "row"), None),
            P(("col", "row"), None),
            P(("row", "col"), None),
            P(("row", "col"), None),
            P(None, ("row", "col")),
        ),
        out_specs=(P(("row", "col"), None), P(("col", "row"), None), P(("col", "row"), None)),
        check_vma=False,
    )
```

```python
import functools
import math

import jax
import jax.numpy as jnp
from jax import lax
from jax.experimental import pallas as pl
from jax.experimental.pallas import tpu as pltpu
from jax.sharding import PartitionSpec as P

H = 4
DH = 128
AXES = ("row", "col")
F32 = jnp.float32
BF16 = jnp.bfloat16
QR = 128
KR = 64
AUX = 16
TILE = 512
HINT = 0.5
LATE = 4 * 10**9
BLK = QR + KR + AUX
QS = 4 * QR
KS = 4 * KR
FACTOR = 1.0 / math.sqrt(DH)
LOG2E = math.log2(math.e)
VMEM = pl.BlockSpec(memory_space=pltpu.VMEM)
HBM = pl.BlockSpec(memory_space=pltpu.HBM)
NT = (((1,), (1,)), ((), ()))


def linear(x, y, z, c):
    return ((z % 2) * 4 + y) * 16 + (z // 2) * 8 + x * 2 + c


def move(value, target):
    pairs = []
    for x in range(4):
        for y in range(4):
            for z in range(4):
                for c in range(2):
                    pairs.append((linear(x, y, z, c), linear(*target(x, y, z, c))))
    return lax.ppermute(value, AXES, pairs)


def other_core(value):
    return move(value, lambda x, y, z, c: (x, y, z, 1 - c))


def partner(place, core, kind):
    if kind == 2:
        return (place + 2) % 4
    up = place % 2 == (kind + core) % 2
    return (place + (1 if up else -1)) % 4


def swap_heads(value, kind):
    return move(value, lambda x, y, z, c: (x, partner(y, c, kind), z, c))


def swap_queries(value, kind):
    return move(value, lambda x, y, z, c: (x, y, partner(z, c, kind), c))


def swap_keys(value, kind):
    return move(value, lambda x, y, z, c: (partner(x, c, kind), y, z, c))


def three_parts(value):
    high = value.astype(BF16).astype(F32)
    rest = value - high
    middle = rest.astype(BF16).astype(F32)
    return [high, middle, rest - middle]


def head_of(kind):
    y = lax.axis_index("row") % 4
    if kind is None:
        return y
    if kind == 2:
        return lax.rem(y + 2, 4)
    odd = lax.rem(y + kind + lax.axis_index("col"), 2)
    return lax.rem(y + 1 + 2 * odd, 4)


def pack_kernel(kinds, *refs):
    count = len(kinds)
    sources, blocks = refs[:6], refs[6 : 6 + count]
    bufs, built, in_sem, out_sem = refs[6 + count : 12 + count], *refs[12 + count :]
    loads = [
        pltpu.make_async_copy(source, buf, in_sem.at[i])
        for i, (source, buf) in enumerate(zip(sources, bufs))
    ]
    for copy in loads:
        copy.start()
    q_buf, k_buf, v_buf, g_buf, o_buf, lse_buf = bufs
    heads = [head_of(kind) for kind in kinds]
    columns = [pl.ds(pl.multiple_of(head * DH, DH), DH) for head in heads]
    sends = []

    def send(j, part, first, rows):
        copy = pltpu.make_async_copy(
            built.at[j, pl.ds(first, rows), :],
            blocks[j].at[pl.ds(first, rows), :],
            out_sem.at[2 * j + part],
        )
        copy.start()
        sends.append(copy)

    for copy in loads[:4]:
        copy.wait()
    for j, cols in enumerate(columns):
        built[j, :QR, :DH] = q_buf[:, cols]
        built[j, :QR, DH:] = g_buf[:, cols]
        built[j, QR : QR + KR, :DH] = k_buf[:, cols]
        built[j, QR : QR + KR, DH:] = v_buf[:, cols]
        send(j, 0, 0, QR + KR)
    for copy in loads[4:]:
        copy.wait()
    for j, (head, cols) in enumerate(zip(heads, columns)):
        product = g_buf[:, cols].astype(F32) * o_buf[:, cols].astype(F32)
        delta = jnp.sum(product.T, axis=0, keepdims=True)
        both = jnp.concatenate([lse_buf[pl.ds(head, 1), :], delta], axis=1)
        rows = three_parts(both) + [jnp.zeros((AUX - 3, 2 * DH), F32)]
        built[j, QR + KR :, :] = jnp.concatenate(rows, axis=0).astype(BF16)
        send(j, 1, QR + KR, AUX)
    for copy in sends:
        copy.wait()


def copy_kernel(source, out):
    out[...] = source[...]


def join_kernel(b2, b0, b1, b3, q_out, kv_out):
    aux = []
    for j, block in enumerate((b0, b1, b2, b3)):
        q_out[j * QR : (j + 1) * QR, :] = block[:QR, :]
        kv_out[j * KR : (j + 1) * KR, :] = block[QR : QR + KR, :]
        aux.append(block[QR + KR :, :].astype(F32)[:3])
    aux.append(jnp.zeros((AUX - 12, 2 * DH), F32))
    q_out[QS:, :] = jnp.concatenate(aux, axis=0).astype(BF16)


def load_queries(blocks, q_all, terms):
    for b, block in enumerate(blocks):
        q_all[b * QS : (b + 1) * QS, :] = block[:QS, :]
        aux = block[QS:, :].astype(F32)
        for j in range(4):
            total = aux[3 * j : 3 * j + 1] + aux[3 * j + 1 : 3 * j + 2] + aux[3 * j + 2 : 3 * j + 3]
            cols = slice(b * QS + j * QR, b * QS + (j + 1) * QR)
            terms[0:1, cols] = total[:, :DH] * LOG2E
            terms[1:2, cols] = total[:, DH:]


def tile_terms(q_all, kv, terms, p_all, ds_all):
    q, g = q_all[:, :DH], q_all[:, DH:]
    s = lax.dot_general(kv[:, :DH], q, NT, preferred_element_type=F32)
    p = jnp.exp2(s * (FACTOR * LOG2E) - terms[0:1, :])
    dp = lax.dot_general(kv[:, DH:], g, NT, preferred_element_type=F32)
    p_all[...] = p.astype(BF16)
    ds_all[...] = (p * (dp - terms[1:2, :]) * FACTOR).astype(BF16)
    dv = jnp.dot(p_all[...], g, preferred_element_type=F32)
    dk = jnp.dot(ds_all[...], q, preferred_element_type=F32)
    dq = jnp.dot(kv[:, :DH].T, ds_all[...], preferred_element_type=F32)
    return dk, dv, dq


def attend_kernel(tiles, old_q, old_kv, *refs):
    refs = list(refs)
    pieces = [refs.pop(0) for _ in range(2 * tiles)]
    blocks = [refs.pop(0) for _ in range(2)]
    dq_old = refs.pop(0) if old_q else None
    dkv_old = [refs.pop(0) for _ in range(tiles)] if old_kv else None
    dkv_out = [refs.pop(0) for _ in range(tiles)]
    q_all, kv, terms, p_all, ds_all = refs[-5:]
    dq_out = refs[:-5]
    load_queries(blocks, q_all, terms)
    total = dq_old[...] if old_q else None
    for i in range(tiles):
        kv[i, :KS, :] = pieces[2 * i][...]
        kv[i, KS:, :] = pieces[2 * i + 1][...]
        dk, dv, dq = tile_terms(q_all, kv.at[i], terms, p_all, ds_all)
        if old_kv:
            dk = dk + dkv_old[i][:, :DH]
            dv = dv + dkv_old[i][:, DH:]
        dkv_out[i][:, :DH] = dk.astype(dkv_out[i].dtype)
        dkv_out[i][:, DH:] = dv.astype(dkv_out[i].dtype)
        total = dq if total is None else total + dq
    if len(dq_out) == 1:
        dq_out[0][...] = total
    else:
        for b, out in enumerate(dq_out):
            out[...] = total[:, b * QS : (b + 1) * QS].T.astype(out.dtype)


def add_kernel(a, b, out):
    out[...] = (a[...].astype(F32) + b[...].astype(F32)).astype(out.dtype)


def split_kernel(*refs):
    own, passed = refs[-2:]
    half = own.shape[0]
    for rows, out in ((slice(0, half), own), (slice(half, 2 * half), passed)):
        total = refs[0][rows, :]
        for ref in refs[1:-2]:
            total = total + ref[rows, :].astype(F32)
        out[...] = total.astype(out.dtype)


def chip_sum_kernel(q3, q0, k0, k1, q1, q2, *outs):
    dq = q0[...] + q1[...].astype(F32) + q2[...].astype(F32) + q3[...].astype(F32)
    dkv = k0[...] + k1[...].astype(F32)
    for j, out in enumerate(outs):
        part = dq[j * QR : (j + 1) * QR]
        wide = jnp.concatenate([part[: QR // 2], part[QR // 2 :]], axis=1)
        out[:KR, :] = wide.astype(out.dtype)
        out[KR:, :] = dkv[j * KR : (j + 1) * KR].astype(out.dtype)


def unpack_kernel(b0, b1, b3, b2, dq, dk, dv):
    for kind, block in ((None, b0), (0, b1), (2, b2), (1, b3)):
        cols = pl.ds(pl.multiple_of(head_of(kind) * DH, DH), DH)
        dq[: QR // 2, cols] = block[:KR, :DH].astype(F32)
        dq[QR // 2 :, cols] = block[:KR, DH:].astype(F32)
        dk[:, cols] = block[KR:, :DH].astype(F32)
        dv[:, cols] = block[KR:, DH:].astype(F32)


def call(kernel, outs, args, scratch=(), flops=0, space=VMEM, out_space=VMEM, limit=40):
    total = sum(a.size * a.dtype.itemsize for a in args) + sum(
        math.prod(shape) * jnp.dtype(kind).itemsize for shape, kind in outs
    )
    return pl.pallas_call(
        kernel,
        out_shape=[jax.ShapeDtypeStruct(shape, kind) for shape, kind in outs],
        in_specs=[space] * len(args),
        out_specs=[out_space] * len(outs),
        scratch_shapes=list(scratch),
        compiler_params=pltpu.CompilerParams(vmem_limit_bytes=limit * 1024 * 1024),
        cost_estimate=pl.CostEstimate(flops=flops, bytes_accessed=total, transcendentals=0),
    )(*args)


def attend(blocks, tiles, dq_old, dkv_old, dq_out, dkv_out):
    args = [piece for tile in tiles for piece in tile] + [*blocks]
    args += ([] if dq_old is None else [dq_old]) + list(dkv_old or ())
    rows = 2 * QS
    outs = call(
        functools.partial(attend_kernel, len(tiles), dq_old is not None, dkv_old is not None),
        [((TILE, 2 * DH), kind) for kind in dkv_out] + dq_out,
        args,
        scratch=[
            pltpu.VMEM((rows, 2 * DH), BF16),
            pltpu.VMEM((len(tiles), TILE, 2 * DH), BF16),
            pltpu.VMEM((8, rows), F32),
            pltpu.VMEM((TILE, rows), BF16),
            pltpu.VMEM((TILE, rows), BF16),
        ],
        flops=int(10 * rows * TILE * len(tiles) * DH * HINT),
    )
    return outs[len(tiles) :], outs[: len(tiles)]


def per_device(queries, keys, values, outputs, d_out, lse):
    args = (queries, keys, values, d_out, outputs, lse)
    with jax.named_scope("pack"):
        def pack(kinds):
            count = len(kinds)
            return call(
                functools.partial(pack_kernel, kinds),
                [((BLK, 2 * DH), BF16)] * count,
                args,
                scratch=[pltpu.VMEM(a.shape, a.dtype) for a in args]
                + [
                    pltpu.VMEM((count, BLK, 2 * DH), BF16),
                    pltpu.SemaphoreType.DMA((6,)),
                    pltpu.SemaphoreType.DMA((2 * count,)),
                ],
                space=HBM,
                out_space=HBM,
                limit=56,
            )

        far, first, second = pack((2, 0, 1))
        here = pack((None,))[0]
        here = call(copy_kernel, [((BLK, 2 * DH), BF16)], (here,))[0]
    with jax.named_scope("heads_to_chips"):
        blocks = [swap_heads(far, 2), here, swap_heads(first, 0), swap_heads(second, 1)]
    with jax.named_scope("join"):
        q, kv = call(join_kernel, [((QS + AUX, 2 * DH), BF16), ((KS, 2 * DH), BF16)], blocks)
    with jax.named_scope("gather_queries"):
        q1 = swap_queries(q, 0)
        q2 = swap_queries(q, 1)
        q3 = swap_queries(q1, 1)
    with jax.named_scope("gather_keys"):
        near = [(kv, swap_keys(kv, 0)), (swap_keys(kv, 1), swap_keys(kv, 2))]
        k_a, k_b = near
        o_a, o_b = [tuple(other_core(piece) for piece in pair) for pair in near]
    sums = [((DH, 2 * QS), F32)]
    q_a = (q, q1)
    q2, k_b = lax.optimization_barrier((q2, k_b))
    with jax.named_scope("attend_a_b"):
        (dq_a,), (dkv_b,) = attend(q_a, (k_b,), None, None, sums, (F32,))
        (dq_a,), (dko_b, dko_a) = attend(q_a, (o_b, o_a), dq_a, None, sums, (F32,) * 2)
    q3, dq_a = lax.optimization_barrier((q3, dq_a))
    q_b = (q2, q3)
    with jax.named_scope("attend_b_b"):
        (dq_b,), (dko_b, dkv_b) = attend(q_b, (o_b, k_b), None, (dko_b, dkv_b), sums, (BF16, F32))
    with jax.named_scope("sum_keys_over_core"):
        sent_b = call(add_kernel, [((TILE, 2 * DH), BF16)], (dkv_b, other_core(dko_b)))[0]
    with jax.named_scope("attend_b_a_other"):
        (dq_b,), (dko_a,) = attend(q_b, (o_a,), dq_b, (dko_a,), sums, (BF16,))
    dq_b, sent_b = lax.optimization_barrier((dq_b, sent_b))
    with jax.named_scope("attend_b_a"):
        (dq2, dq3), (dkv_a,) = attend(q_b, (k_a,), dq_b, None, [((QS, DH), BF16)] * 2, (F32,))
    with jax.named_scope("sum_queries"):
        got2, got3 = swap_queries(dq2, 1), swap_queries(dq3, 2)
    with jax.named_scope("sum_keys"):
        got_b = swap_keys(sent_b, 1)
    with jax.named_scope("sum_keys_over_core"):
        got_other = other_core(dko_a)
    with jax.named_scope("attend_a_a"):
        (dq0, dq1), (dkv_own,) = attend(
            q_a, (k_a,), dq_a, (dkv_a,), [((QS, DH), F32), ((QS, DH), BF16)], (F32,)
        )
    with jax.named_scope("sum_queries"):
        got1 = swap_queries(dq1, 0)
        got3 = call(copy_kernel, [((QS, DH), BF16)], (got3,), flops=LATE)[0]
    with jax.named_scope("sum_keys"):
        k_own, k_sent = call(
            split_kernel, [((KS, 2 * DH), F32), ((KS, 2 * DH), BF16)], (dkv_own, got_other, got_b)
        )
        k_got = swap_keys(k_sent, 0)
    with jax.named_scope("chip_sum"):
        backs = call(
            chip_sum_kernel,
            [((2 * KR, 2 * DH), F32)] + [((2 * KR, 2 * DH), BF16)] * 3,
            (got3, dq0, k_own, k_got, got1, got2),
        )
    with jax.named_scope("back_to_rows"):
        far = swap_heads(backs[2], 2)
        backs = [backs[0], swap_heads(backs[1], 0), swap_heads(backs[3], 1), far]
    with jax.named_scope("unpack"):
        return tuple(
            call(
                unpack_kernel,
                [((QR, H * DH), F32), ((KR, H * DH), F32), ((KR, H * DH), F32)],
                backs,
            )
        )


def solution(mesh):
    return jax.shard_map(
        per_device,
        mesh=mesh,
        in_specs=(
            P(("row", "col"), None),
            P(("col", "row"), None),
            P(("col", "row"), None),
            P(("row", "col"), None),
            P(("row", "col"), None),
            P(None, ("row", "col")),
        ),
        out_specs=(P(("row", "col"), None), P(("col", "row"), None), P(("col", "row"), None)),
        check_vma=False,
    )
```

```python
import functools
import math

import jax
import jax.numpy as jnp
from jax import lax
from jax.experimental import pallas as pl
from jax.experimental.pallas import tpu as pltpu
from jax.sharding import PartitionSpec as P

H = 4
DH = 128
AXES = ("row", "col")
F32 = jnp.float32
BF16 = jnp.bfloat16
QR = 128
KR = 64
AUX = 16
TILE = 512
HINT = 0.5
LATE = 4 * 10**9
BLK = QR + KR + AUX
QS = 4 * QR
KS = 4 * KR
FACTOR = 1.0 / math.sqrt(DH)
LOG2E = math.log2(math.e)
VMEM = pl.BlockSpec(memory_space=pltpu.VMEM)
HBM = pl.BlockSpec(memory_space=pltpu.HBM)
NT = (((1,), (1,)), ((), ()))


def linear(x, y, z, c):
    return ((z % 2) * 4 + y) * 16 + (z // 2) * 8 + x * 2 + c


def move(value, target):
    pairs = []
    for x in range(4):
        for y in range(4):
            for z in range(4):
                for c in range(2):
                    pairs.append((linear(x, y, z, c), linear(*target(x, y, z, c))))
    return lax.ppermute(value, AXES, pairs)


def other_core(value):
    return move(value, lambda x, y, z, c: (x, y, z, 1 - c))


def partner(place, core, kind):
    if kind == 2:
        return (place + 2) % 4
    up = place % 2 == (kind + core) % 2
    return (place + (1 if up else -1)) % 4


def swap_heads(value, kind):
    return move(value, lambda x, y, z, c: (x, partner(y, c, kind), z, c))


def swap_queries(value, kind):
    return move(value, lambda x, y, z, c: (x, y, partner(z, c, kind), c))


def swap_keys(value, kind):
    return move(value, lambda x, y, z, c: (partner(x, c, kind), y, z, c))


def three_parts(value):
    high = value.astype(BF16).astype(F32)
    rest = value - high
    middle = rest.astype(BF16).astype(F32)
    return [high, middle, rest - middle]


def head_of(kind):
    y = lax.axis_index("row") % 4
    if kind is None:
        return y
    if kind == 2:
        return lax.rem(y + 2, 4)
    odd = lax.rem(y + kind + lax.axis_index("col"), 2)
    return lax.rem(y + 1 + 2 * odd, 4)


def pack_kernel(kinds, *refs):
    count = len(kinds)
    sources, blocks = refs[:6], refs[6 : 6 + count]
    bufs, built, in_sem, out_sem = refs[6 + count : 12 + count], *refs[12 + count :]
    loads = [
        pltpu.make_async_copy(source, buf, in_sem.at[i])
        for i, (source, buf) in enumerate(zip(sources, bufs))
    ]
    for copy in loads:
        copy.start()
    q_buf, k_buf, v_buf, g_buf, o_buf, lse_buf = bufs
    heads = [head_of(kind) for kind in kinds]
    columns = [pl.ds(pl.multiple_of(head * DH, DH), DH) for head in heads]
    sends = []

    def send(j, part, first, rows):
        copy = pltpu.make_async_copy(
            built.at[j, pl.ds(first, rows), :],
            blocks[j].at[pl.ds(first, rows), :],
            out_sem.at[2 * j + part],
        )
        copy.start()
        sends.append(copy)

    for copy in loads[:4]:
        copy.wait()
    for j, cols in enumerate(columns):
        built[j, :QR, :DH] = q_buf[:, cols]
        built[j, :QR, DH:] = g_buf[:, cols]
        built[j, QR : QR + KR, :DH] = k_buf[:, cols]
        built[j, QR : QR + KR, DH:] = v_buf[:, cols]
        send(j, 0, 0, QR + KR)
    for copy in loads[4:]:
        copy.wait()
    for j, (head, cols) in enumerate(zip(heads, columns)):
        product = g_buf[:, cols].astype(F32) * o_buf[:, cols].astype(F32)
        delta = jnp.sum(product.T, axis=0, keepdims=True)
        both = jnp.concatenate([lse_buf[pl.ds(head, 1), :], delta], axis=1)
        rows = three_parts(both) + [jnp.zeros((AUX - 3, 2 * DH), F32)]
        built[j, QR + KR :, :] = jnp.concatenate(rows, axis=0).astype(BF16)
        send(j, 1, QR + KR, AUX)
    for copy in sends:
        copy.wait()


def copy_kernel(source, out):
    out[...] = source[...]


def join_kernel(b2, b0, b1, b3, q_out, kv_out):
    aux = []
    for j, block in enumerate((b0, b1, b2, b3)):
        q_out[j * QR : (j + 1) * QR, :] = block[:QR, :]
        kv_out[j * KR : (j + 1) * KR, :] = block[QR : QR + KR, :]
        aux.append(block[QR + KR :, :].astype(F32)[:3])
    aux.append(jnp.zeros((AUX - 12, 2 * DH), F32))
    q_out[QS:, :] = jnp.concatenate(aux, axis=0).astype(BF16)


def load_queries(blocks, q_all, terms):
    for b, block in enumerate(blocks):
        q_all[b * QS : (b + 1) * QS, :] = block[:QS, :]
        aux = block[QS:, :].astype(F32)
        for j in range(4):
            total = aux[3 * j : 3 * j + 1] + aux[3 * j + 1 : 3 * j + 2] + aux[3 * j + 2 : 3 * j + 3]
            cols = slice(b * QS + j * QR, b * QS + (j + 1) * QR)
            terms[0:1, cols] = total[:, :DH] * LOG2E
            terms[1:2, cols] = total[:, DH:]


def tile_terms(q_all, kv, terms, p_all, ds_all):
    q, g = q_all[:, :DH], q_all[:, DH:]
    s = lax.dot_general(kv[:, :DH], q, NT, preferred_element_type=F32)
    p = jnp.exp2(s * (FACTOR * LOG2E) - terms[0:1, :])
    dp = lax.dot_general(kv[:, DH:], g, NT, preferred_element_type=F32)
    p_all[...] = p.astype(BF16)
    ds_all[...] = (p * (dp - terms[1:2, :]) * FACTOR).astype(BF16)
    dv = jnp.dot(p_all[...], g, preferred_element_type=F32)
    dk = jnp.dot(ds_all[...], q, preferred_element_type=F32)
    dq = jnp.dot(kv[:, :DH].T, ds_all[...], preferred_element_type=F32)
    return dk, dv, dq


def attend_kernel(tiles, old_q, old_kv, *refs):
    refs = list(refs)
    pieces = [refs.pop(0) for _ in range(2 * tiles)]
    blocks = [refs.pop(0) for _ in range(2)]
    dq_old = refs.pop(0) if old_q else None
    dkv_old = [refs.pop(0) for _ in range(tiles)] if old_kv else None
    dkv_out = [refs.pop(0) for _ in range(tiles)]
    q_all, kv, terms, p_all, ds_all = refs[-5:]
    dq_out = refs[:-5]
    load_queries(blocks, q_all, terms)
    total = dq_old[...] if old_q else None
    for i in range(tiles):
        kv[i, :KS, :] = pieces[2 * i][...]
        kv[i, KS:, :] = pieces[2 * i + 1][...]
        dk, dv, dq = tile_terms(q_all, kv.at[i], terms, p_all, ds_all)
        if old_kv:
            dk = dk + dkv_old[i][:, :DH]
            dv = dv + dkv_old[i][:, DH:]
        dkv_out[i][:, :DH] = dk.astype(dkv_out[i].dtype)
        dkv_out[i][:, DH:] = dv.astype(dkv_out[i].dtype)
        total = dq if total is None else total + dq
    if len(dq_out) == 1:
        dq_out[0][...] = total
    else:
        for b, out in enumerate(dq_out):
            out[...] = total[:, b * QS : (b + 1) * QS].T.astype(out.dtype)


def add_kernel(a, b, out):
    out[...] = (a[...].astype(F32) + b[...].astype(F32)).astype(out.dtype)


def split_kernel(*refs):
    own, passed = refs[-2:]
    half = own.shape[0]
    for rows, out in ((slice(0, half), own), (slice(half, 2 * half), passed)):
        total = refs[0][rows, :]
        for ref in refs[1:-2]:
            total = total + ref[rows, :].astype(F32)
        out[...] = total.astype(out.dtype)


def chip_sum_kernel(q23, q0, k0, k1, q1, *outs):
    dq = q0[...] + q1[...].astype(F32) + q23[...]
    dkv = k0[...] + k1[...].astype(F32)
    for j, out in enumerate(outs):
        part = dq[j * QR : (j + 1) * QR]
        wide = jnp.concatenate([part[: QR // 2], part[QR // 2 :]], axis=1)
        out[:KR, :] = wide.astype(out.dtype)
        out[KR:, :] = dkv[j * KR : (j + 1) * KR].astype(out.dtype)


def unpack_kernel(b0, b1, b3, b2, dq, dk, dv):
    for kind, block in ((None, b0), (0, b1), (2, b2), (1, b3)):
        cols = pl.ds(pl.multiple_of(head_of(kind) * DH, DH), DH)
        dq[: QR // 2, cols] = block[:KR, :DH].astype(F32)
        dq[QR // 2 :, cols] = block[:KR, DH:].astype(F32)
        dk[:, cols] = block[KR:, :DH].astype(F32)
        dv[:, cols] = block[KR:, DH:].astype(F32)


def call(kernel, outs, args, scratch=(), flops=0, space=VMEM, out_space=VMEM, limit=40):
    total = sum(a.size * a.dtype.itemsize for a in args) + sum(
        math.prod(shape) * jnp.dtype(kind).itemsize for shape, kind in outs
    )
    return pl.pallas_call(
        kernel,
        out_shape=[jax.ShapeDtypeStruct(shape, kind) for shape, kind in outs],
        in_specs=[space] * len(args),
        out_specs=[out_space] * len(outs),
        scratch_shapes=list(scratch),
        compiler_params=pltpu.CompilerParams(vmem_limit_bytes=limit * 1024 * 1024),
        cost_estimate=pl.CostEstimate(flops=flops, bytes_accessed=total, transcendentals=0),
    )(*args)


def attend(blocks, tiles, dq_old, dkv_old, dq_out, dkv_out):
    args = [piece for tile in tiles for piece in tile] + [*blocks]
    args += ([] if dq_old is None else [dq_old]) + list(dkv_old or ())
    rows = 2 * QS
    outs = call(
        functools.partial(attend_kernel, len(tiles), dq_old is not None, dkv_old is not None),
        [((TILE, 2 * DH), kind) for kind in dkv_out] + dq_out,
        args,
        scratch=[
            pltpu.VMEM((rows, 2 * DH), BF16),
            pltpu.VMEM((len(tiles), TILE, 2 * DH), BF16),
            pltpu.VMEM((8, rows), F32),
            pltpu.VMEM((TILE, rows), BF16),
            pltpu.VMEM((TILE, rows), BF16),
        ],
        flops=int(10 * rows * TILE * len(tiles) * DH * HINT),
    )
    return outs[len(tiles) :], outs[: len(tiles)]


def per_device(queries, keys, values, outputs, d_out, lse):
    args = (queries, keys, values, d_out, outputs, lse)
    with jax.named_scope("pack"):
        def pack(kinds):
            count = len(kinds)
            return call(
                functools.partial(pack_kernel, kinds),
                [((BLK, 2 * DH), BF16)] * count,
                args,
                scratch=[pltpu.VMEM(a.shape, a.dtype) for a in args]
                + [
                    pltpu.VMEM((count, BLK, 2 * DH), BF16),
                    pltpu.SemaphoreType.DMA((6,)),
                    pltpu.SemaphoreType.DMA((2 * count,)),
                ],
                space=HBM,
                out_space=HBM,
                limit=56,
            )

        far, first, second = pack((2, 0, 1))
        here = pack((None,))[0]
        here = call(copy_kernel, [((BLK, 2 * DH), BF16)], (here,))[0]
    with jax.named_scope("heads_to_chips"):
        blocks = [swap_heads(far, 2), here, swap_heads(first, 0), swap_heads(second, 1)]
    with jax.named_scope("join"):
        q, kv = call(join_kernel, [((QS + AUX, 2 * DH), BF16), ((KS, 2 * DH), BF16)], blocks)
    with jax.named_scope("gather_queries"):
        q1 = swap_queries(q, 0)
        q2 = swap_queries(q, 1)
        q3 = swap_queries(q1, 1)
    with jax.named_scope("gather_keys"):
        near = [(kv, swap_keys(kv, 0)), (swap_keys(kv, 1), swap_keys(kv, 2))]
        k_a, k_b = near
        o_a, o_b = [tuple(other_core(piece) for piece in pair) for pair in near]
    sums = [((DH, 2 * QS), F32)]
    q_a = (q, q1)
    q2, k_b = lax.optimization_barrier((q2, k_b))
    with jax.named_scope("attend_a_b"):
        (dq_a,), (dkv_b,) = attend(q_a, (k_b,), None, None, sums, (F32,))
        (dq_a,), (dko_b, dko_a) = attend(q_a, (o_b, o_a), dq_a, None, sums, (F32,) * 2)
    q3, dq_a = lax.optimization_barrier((q3, dq_a))
    q_b = (q2, q3)
    with jax.named_scope("attend_b_b"):
        (dq_b,), (dko_b, dkv_b) = attend(q_b, (o_b, k_b), None, (dko_b, dkv_b), sums, (BF16, F32))
    with jax.named_scope("sum_keys_over_core"):
        sent_b = call(add_kernel, [((TILE, 2 * DH), BF16)], (dkv_b, other_core(dko_b)))[0]
    with jax.named_scope("attend_b_a_other"):
        (dq_b,), (dko_a,) = attend(q_b, (o_a,), dq_b, (dko_a,), sums, (BF16,))
    dq_b, sent_b = lax.optimization_barrier((dq_b, sent_b))
    with jax.named_scope("attend_b_a"):
        (dq2, dq3), (dkv_a,) = attend(q_b, (k_a,), dq_b, None, [((QS, DH), BF16)] * 2, (F32,))
    with jax.named_scope("sum_queries"):
        got2, got3 = swap_queries(dq2, 1), swap_queries(dq3, 2)
    with jax.named_scope("sum_keys"):
        got_b = swap_keys(sent_b, 1)
    with jax.named_scope("sum_keys_over_core"):
        got_other = other_core(dko_a)
    with jax.named_scope("attend_a_a"):
        (dq0, dq1), (dkv_own,) = attend(
            q_a, (k_a,), dq_a, (dkv_a,), [((QS, DH), F32), ((QS, DH), BF16)], (F32,)
        )
    with jax.named_scope("sum_queries"):
        got1 = swap_queries(dq1, 0)
        got23 = call(add_kernel, [((QS, DH), F32)], (got2, got3), flops=LATE)[0]
    with jax.named_scope("sum_keys"):
        k_own, k_sent = call(
            split_kernel, [((KS, 2 * DH), F32), ((KS, 2 * DH), BF16)], (dkv_own, got_other, got_b)
        )
        k_got = swap_keys(k_sent, 0)
    with jax.named_scope("chip_sum"):
        backs = call(
            chip_sum_kernel,
            [((2 * KR, 2 * DH), F32)] + [((2 * KR, 2 * DH), BF16)] * 3,
            (got23, dq0, k_own, k_got, got1),
        )
    with jax.named_scope("back_to_rows"):
        far = swap_heads(backs[2], 2)
        backs = [backs[0], swap_heads(backs[1], 0), swap_heads(backs[3], 1), far]
    with jax.named_scope("unpack"):
        return tuple(
            call(
                unpack_kernel,
                [((QR, H * DH), F32), ((KR, H * DH), F32), ((KR, H * DH), F32)],
                backs,
            )
        )


def solution(mesh):
    return jax.shard_map(
        per_device,
        mesh=mesh,
        in_specs=(
            P(("row", "col"), None),
            P(("col", "row"), None),
            P(("col", "row"), None),
            P(("row", "col"), None),
            P(("row", "col"), None),
            P(None, ("row", "col")),
        ),
        out_specs=(P(("row", "col"), None), P(("col", "row"), None), P(("col", "row"), None)),
        check_vma=False,
    )
```
